32 devices in a mesh: chan: 4 (over z), row: 4 (over y, core), col: 2 (over x).
Axes of the slice: x: 2, y: 2, z: 4, core: 2. Of those that a mesh axis runs over, the one named last changes fastest.
Arguments:
- voltages: bfloat16 [1024, 262144], P('chan', ('row', 'col')), may hold values from -6 to 6
Outputs:
- visibilities: float32 [256, 2, 1024, 1024], P('chan', None, 'row', 'col')
The draws below stay inside these ranges and needn't reach their ends.
All inputs are finite; a program needn't handle non-finite values.
Results may differ from the reference program's by a relative error of at most 0.0053.
Values may be sent and summed in bfloat16 or wider, within the bound.
A program may use at most 384 MiB of HBM per device.

```python
import jax
import jax.numpy as jnp
from jax import lax

INPUTS = 1024
FFT_LEN = 512
TAPS = 8
CHANNELS = 256
SPECTRA = 512
N_CHAN = 4


def shard_levels(rng, dims, shards, low, largest):
    factor_of, own = 1.0, jax.random.fold_in(rng, 6)
    for dim, blocks in shards:
        heights = jnp.exp(jax.random.uniform(jax.random.fold_in(own, dim), (blocks,), jnp.float32, low / len(shards), largest / len(shards)))
        factor_of = factor_of * jnp.repeat(heights, dims[dim] // blocks).reshape([-1 if axis == dim else 1 for axis in range(len(dims))])
    return factor_of


def gaussian(own_key, shape, spread, bound, cuts=(), kind=jnp.bfloat16):
    level = shard_levels(own_key, shape, cuts, -0.22, 0.18) if cuts else 1.0
    drawn = jax.random.normal(own_key, shape, jnp.float32) * spread * level
    return jnp.minimum(jnp.maximum(drawn, -bound), bound).astype(kind)


def setup_inputs(seed: int = 0) -> dict:
    key_list = jax.random.split(jax.random.key(seed), 2)
    return {
        "voltages": gaussian(key_list[0], (INPUTS, SPECTRA * FFT_LEN), 1.0, 6.0, ((0, 4), (1, 8))),
    }


def window_table(taps, length):
    count = taps * length
    position = jnp.arange(count).astype(jnp.float32)
    offset = (position - count / 2 + 0.5) / length
    taper = 0.5 - 0.5 * jnp.cos(2.0 * jnp.pi * (position + 0.5) / count)
    values = jnp.sinc(offset) * taper
    values = values / jnp.sqrt(jnp.sum(values * values))
    return values.reshape(taps, length)

def fourier_table(channels, length):
    channel_index = jnp.arange(channels, dtype=jnp.int32)[:, None]
    sample_index = jnp.arange(length, dtype=jnp.int32)[None, :]
    phase = (channel_index * sample_index % length).astype(jnp.float32) * (2.0 * jnp.pi / length)
    return jnp.stack([jnp.cos(phase), -jnp.sin(phase)], axis=1).astype(jnp.bfloat16)

def reference(voltages):
    window = window_table(TAPS, FFT_LEN)
    table = fourier_table(CHANNELS, FFT_LEN).astype(jnp.float32)
    group = INPUTS // N_CHAN
    grouped = voltages.reshape(N_CHAN, group, SPECTRA * FFT_LEN)

    def analyse(block):
        zeros = jnp.zeros((group, (TAPS - 1) * FFT_LEN), jnp.bfloat16)
        padded = jnp.concatenate([zeros, block], axis=1).reshape(group, SPECTRA + TAPS - 1, FFT_LEN)
        total = jnp.zeros((group, SPECTRA, FFT_LEN), jnp.float32)
        for tap_index in range(TAPS):
            total = total + window[tap_index][None, None, :] * padded[:, tap_index:tap_index + SPECTRA, :].astype(jnp.float32)
        filtered = total.astype(jnp.bfloat16).astype(jnp.float32)
        spectra = jnp.einsum('kpn,isn->kpsi', table, filtered, precision=lax.Precision.HIGHEST)
        return spectra.astype(jnp.bfloat16)
    pieces = lax.map(analyse, grouped)
    spectra = jnp.transpose(pieces, (1, 2, 3, 0, 4)).reshape(CHANNELS, 2, SPECTRA, INPUTS)

    def correlate(single):
        values = single.astype(jnp.float32)
        stacked = values.reshape(2 * SPECTRA, INPUTS)
        flipped = jnp.concatenate([values[1], -values[0]], axis=0)
        real_part = jnp.dot(stacked.T, stacked, precision=lax.Precision.HIGHEST)
        imag_part = jnp.dot(flipped.T, stacked, precision=lax.Precision.HIGHEST)
        return jnp.stack([real_part, imag_part], axis=0) / SPECTRA
    return lax.map(correlate, spectra)
```

```python
import functools

import jax
import jax.numpy as jnp
from jax import lax
from jax.experimental import pallas as pl
from jax.experimental.pallas import tpu as pltpu
from jax.sharding import PartitionSpec as P

FFT_LEN = 512
TAPS = 8
CHANNELS = 256
CHUNKS = 8
STEP = 16
ROWS = 32
HALO = (TAPS - 1) * FFT_LEN


def shifted(value, axis, by):
    length = lax.axis_size(axis)
    pairs = [(i, i + by) for i in range(length) if 0 <= i + by < length]
    return lax.ppermute(value, axis, pairs)


def window_table(taps, length):
    count = taps * length
    position = jnp.arange(count).astype(jnp.float32)
    offset = (position - count / 2 + 0.5) / length
    taper = 0.5 - 0.5 * jnp.cos(2.0 * jnp.pi * (position + 0.5) / count)
    values = jnp.sinc(offset) * taper
    values = values / jnp.sqrt(jnp.sum(values * values))
    return values.reshape(taps, length)


def fourier_table(channels, length):
    channel_index = jnp.arange(channels, dtype=jnp.int32)[:, None]
    sample_index = jnp.arange(length, dtype=jnp.int32)[None, :]
    phase = (channel_index * sample_index % length).astype(jnp.float32) * (2.0 * jnp.pi / length)
    return jnp.stack([jnp.cos(phase), -jnp.sin(phase)], axis=1).astype(jnp.bfloat16)


def filter_kernel(halo_ref, volt_ref, window_ref, table_ref, *rest):
    outs, (ext, filt, turned) = rest[:-3], rest[-3:]
    inputs = volt_ref.shape[0]
    span = STEP * FFT_LEN

    @pl.when(pl.program_id(0) == 0)
    def _():
        ext[:, :HALO] = halo_ref[...]

    @pl.when(pl.program_id(0) > 0)
    def _():
        ext[:, :HALO] = ext[:, span : span + HALO]

    ext[:, HALO:] = volt_ref[...]

    @pl.loop(0, STEP)
    def _(s):
        for row in range(0, inputs, ROWS):
            total = jnp.zeros((ROWS, FFT_LEN), jnp.float32)
            for tap in range(TAPS):
                start = pl.multiple_of((s + tap) * FFT_LEN, FFT_LEN)
                block = ext[row : row + ROWS, pl.ds(start, FFT_LEN)]
                total = total + window_ref[tap : tap + 1, :] * block.astype(jnp.float32)
            filt[row : row + ROWS, :] = total.astype(jnp.bfloat16)
        spectrum = lax.dot_general(
            table_ref[...], filt[...], (((1,), (1,)), ((), ())), preferred_element_type=jnp.float32
        )
        for lane in range(inputs // 128):
            turned[lane, pl.ds(s, spectrum.shape[0], stride=STEP), :] = spectrum[:, lane * 128 : (lane + 1) * 128]

    count = turned.shape[1] // len(outs)
    for chunk, out in enumerate(outs):
        for lane in range(inputs // 128):
            piece = turned[lane, chunk * count : (chunk + 1) * count, :].astype(jnp.bfloat16)
            out[..., lane * 128 : (lane + 1) * 128] = piece.reshape(out.shape[:-1] + (128,))


def filter_and_transform(halo, voltages, window, table, groups):
    inputs, samples = voltages.shape
    slots = samples // FFT_LEN
    rows = table.shape[0]
    width = CHANNELS // groups // CHUNKS
    shape = (groups, width, 2, slots, inputs)
    return pl.pallas_call(
        filter_kernel,
        grid=(slots // STEP,),
        in_specs=[
            pl.BlockSpec((inputs, HALO), lambda j: (0, 0)),
            pl.BlockSpec((inputs, STEP * FFT_LEN), lambda j: (0, j)),
            pl.BlockSpec((TAPS, FFT_LEN), lambda j: (0, 0)),
            pl.BlockSpec((rows, FFT_LEN), lambda j: (0, 0)),
        ],
        out_specs=[pl.BlockSpec((groups, width, 2, STEP, inputs), lambda j: (0, 0, 0, j, 0))] * CHUNKS,
        out_shape=[jax.ShapeDtypeStruct(shape, jnp.bfloat16)] * CHUNKS,
        scratch_shapes=[
            pltpu.VMEM((inputs, HALO + STEP * FFT_LEN), jnp.bfloat16),
            pltpu.VMEM((inputs, FFT_LEN), jnp.bfloat16),
            pltpu.VMEM((inputs // 128, rows * STEP, 128), jnp.float32),
        ],
        compiler_params=pltpu.CompilerParams(vmem_limit_bytes=50 * 2**20),
        name="filter_and_transform",
    )(halo, voltages, window, table)


def tile_kernel(scale, place_ref, left_ref, right_ref, *rest):
    out = rest[-1]
    devices, _, _, parts, slots, inputs = left_ref.shape

    def matrix(ref, index, part):
        return ref[:, index, 0, part].reshape(devices * slots, inputs)

    def product(left, right):
        return lax.dot_general(left, right, (((0,), (0,)), ((), ())), preferred_element_type=jnp.float32)

    for i in range(left_ref.shape[1]):
        rows = slice(i * inputs, (i + 1) * inputs)
        left = [matrix(left_ref, i, 0), matrix(left_ref, i, 1)]
        for j in range(right_ref.shape[1]):
            columns = slice(j * inputs, (j + 1) * inputs)
            right = [matrix(right_ref, j, 0), matrix(right_ref, j, 1)]
            out[0, 0, rows, columns] = (product(left[0], right[0]) + product(left[1], right[1])) * scale
            out[0, 1, rows, columns] = (product(left[1], right[0]) - product(left[0], right[1])) * scale


def tiles(piece, place, before, chunk, shape, scale):
    devices, groups, width, parts, slots, inputs = piece.shape
    rows, columns = shape[2] // inputs, shape[3] // inputs
    in_specs = [
        pl.BlockSpec((devices, rows, 1, parts, slots, inputs), lambda k, at: (0, at[0], k, 0, 0, 0)),
        pl.BlockSpec((devices, columns, 1, parts, slots, inputs), lambda k, at: (0, at[1], k, 0, 0, 0)),
    ]
    operands = [place, piece, piece]
    aliases = {}
    if before is not None:
        in_specs.append(pl.BlockSpec(memory_space=pl.ANY))
        operands.append(before)
        aliases = {3: 0}
    moved = (rows + columns) * devices * width * parts * slots * inputs * 2
    return pl.pallas_call(
        functools.partial(tile_kernel, scale),
        grid_spec=pltpu.PrefetchScalarGridSpec(
            num_scalar_prefetch=1,
            grid=(width,),
            in_specs=in_specs,
            out_specs=pl.BlockSpec((1,) + shape[1:], lambda k, at: (chunk * width + k, 0, 0, 0)),
        ),
        out_shape=jax.ShapeDtypeStruct(shape, jnp.float32),
        input_output_aliases=aliases,
        cost_estimate=pl.CostEstimate(
            flops=8 * width * devices * slots * shape[2] * shape[3],
            bytes_accessed=moved + width * 2 * shape[2] * shape[3] * 4,
            transcendentals=0,
        ),
        compiler_params=pltpu.CompilerParams(vmem_limit_bytes=56 * 2**20),
        name="visibility_tiles",
    )(*operands)


def chunked(voltages):
    samples = voltages.shape[1]
    groups = lax.axis_size("chan")
    table = fourier_table(CHANNELS, FFT_LEN)
    table = table.reshape(groups, CHUNKS, CHANNELS // groups // CHUNKS, 2, FFT_LEN)
    table = table.transpose(1, 0, 2, 3, 4).reshape(2 * CHANNELS, FFT_LEN)
    window = window_table(TAPS, FFT_LEN)
    halo = shifted(voltages[:, samples - HALO :], ("row", "col"), 1)
    chunks = filter_and_transform(halo, voltages, window, table, groups)
    row_count = lax.axis_size("row")
    col_count = lax.axis_size("col")
    total_inputs = voltages.shape[0] * groups
    spectra_total = samples // FFT_LEN * row_count * col_count
    place = jnp.stack([lax.axis_index("row"), lax.axis_index("col")]).astype(jnp.int32)
    shape = (CHANNELS // groups, 2, total_inputs // row_count, total_inputs // col_count)
    out = None
    for index, chunk in enumerate(chunks):
        turned = lax.all_to_all(chunk, "chan", split_axis=0, concat_axis=0, tiled=True)
        piece = lax.all_gather(turned, ("row", "col"), axis=0, tiled=False)
        out = tiles(piece, place, out, index, shape, 1.0 / spectra_total)
    return out


def whole(voltages):
    local_inputs = voltages.shape[0]
    slot_spectra = voltages.shape[1] // FFT_LEN
    window = window_table(TAPS, FFT_LEN)
    table = fourier_table(CHANNELS, FFT_LEN)
    earlier = shifted(voltages[:, (slot_spectra - TAPS + 1) * FFT_LEN :], ("row", "col"), 1)
    extended = jnp.concatenate([earlier, voltages], axis=1).reshape(
        local_inputs, slot_spectra + TAPS - 1, FFT_LEN
    )
    total = jnp.zeros((local_inputs, slot_spectra, FFT_LEN), jnp.float32)
    for tap_index in range(TAPS):
        total = total + window[tap_index][None, None, :] * extended[
            :, tap_index : tap_index + slot_spectra, :
        ].astype(jnp.float32)
    filtered = total.astype(jnp.bfloat16)
    spectra = jnp.einsum(
        "kpn,isn->kpsi", table, filtered, preferred_element_type=jnp.float32
    ).astype(jnp.bfloat16)
    turned = lax.all_to_all(spectra, "chan", split_axis=0, concat_axis=3, tiled=True)
    inputs_all = turned.shape[3]
    row_count = lax.axis_size("row")
    col_count = lax.axis_size("col")
    row_block = inputs_all // row_count
    col_block = inputs_all // col_count
    spectra_total = slot_spectra * row_count * col_count
    piece = lax.all_gather(turned, ("row", "col"), axis=2, tiled=True)
    left = lax.dynamic_slice_in_dim(piece, lax.axis_index("row") * row_block, row_block, 3)
    right = lax.dynamic_slice_in_dim(piece, lax.axis_index("col") * col_block, col_block, 3)
    flipped = jnp.stack([left[:, 1], -left[:, 0]], axis=1)
    real_part = jnp.einsum("cpsi,cpsj->cij", left, right, preferred_element_type=jnp.float32)
    imag_part = jnp.einsum("cpsi,cpsj->cij", flipped, right, preferred_element_type=jnp.float32)
    return jnp.stack([real_part, imag_part], axis=1) / spectra_total


def per_device(voltages):
    inputs, samples = voltages.shape
    groups = lax.axis_size("chan")
    row_block = inputs * groups // lax.axis_size("row")
    col_block = inputs * groups // lax.axis_size("col")
    fits = inputs % 128 == 0 and row_block % inputs == 0 and col_block % inputs == 0
    fits = fits and CHANNELS % (groups * CHUNKS) == 0 and samples % (STEP * FFT_LEN) == 0
    return chunked(voltages) if fits else whole(voltages)


def solution(mesh):
    placed = (P("chan", ("row", "col")),)
    return jax.shard_map(
        per_device,
        mesh=mesh,
        in_specs=placed,
        out_specs=P("chan", None, "row", "col"),
        check_vma=False,
    )
```

```python
import functools

import jax
import jax.numpy as jnp
from jax import lax
from jax.experimental import pallas as pl
from jax.experimental.pallas import tpu as pltpu
from jax.sharding import PartitionSpec as P

FFT_LEN = 512
TAPS = 8
CHANNELS = 256
PARTS = (1, 2, 3, 2)
EIGHTHS = sum(PARTS)
STEP = 16
ROWS = 32
HALO = (TAPS - 1) * FFT_LEN


def shifted(value, axis, by):
    length = lax.axis_size(axis)
    pairs = [(i, i + by) for i in range(length) if 0 <= i + by < length]
    return lax.ppermute(value, axis, pairs)


def window_table(taps, length):
    count = taps * length
    position = jnp.arange(count).astype(jnp.float32)
    offset = (position - count / 2 + 0.5) / length
    taper = 0.5 - 0.5 * jnp.cos(2.0 * jnp.pi * (position + 0.5) / count)
    values = jnp.sinc(offset) * taper
    values = values / jnp.sqrt(jnp.sum(values * values))
    return values.reshape(taps, length)


def fourier_table(channels, length):
    channel_index = jnp.arange(channels, dtype=jnp.int32)[:, None]
    sample_index = jnp.arange(length, dtype=jnp.int32)[None, :]
    phase = (channel_index * sample_index % length).astype(jnp.float32) * (2.0 * jnp.pi / length)
    return jnp.stack([jnp.cos(phase), -jnp.sin(phase)], axis=1).astype(jnp.bfloat16)


def filter_kernel(halo_ref, volt_ref, window_ref, table_ref, *rest):
    outs, (ext, filt, turned) = rest[-3 - len(PARTS) : -3], rest[-3:]
    inputs = volt_ref.shape[0]
    span = STEP * FFT_LEN

    @pl.when(pl.program_id(0) == 0)
    def _():
        ext[:, :HALO] = halo_ref[...]

    @pl.when(pl.program_id(0) > 0)
    def _():
        ext[:, :HALO] = ext[:, span : span + HALO]

    ext[:, HALO:] = volt_ref[...]

    @pl.loop(0, STEP)
    def _(s):
        for row in range(0, inputs, ROWS):
            total = jnp.zeros((ROWS, FFT_LEN), jnp.float32)
            for tap in range(TAPS):
                start = pl.multiple_of((s + tap) * FFT_LEN, FFT_LEN)
                block = ext[row : row + ROWS, pl.ds(start, FFT_LEN)]
                total = total + window_ref[tap : tap + 1, :] * block.astype(jnp.float32)
            filt[row : row + ROWS, :] = total.astype(jnp.bfloat16)
        spectrum = lax.dot_general(
            table_ref[...], filt[...], (((1,), (1,)), ((), ())), preferred_element_type=jnp.float32
        )
        for lane in range(inputs // 128):
            turned[lane, pl.ds(s, spectrum.shape[0], stride=STEP), :] = spectrum[:, lane * 128 : (lane + 1) * 128]

    unit = turned.shape[1] // EIGHTHS
    for chunk, out in enumerate(outs):
        first, last = sum(PARTS[:chunk]) * unit, sum(PARTS[: chunk + 1]) * unit
        for lane in range(inputs // 128):
            piece = turned[lane, first:last, :].astype(jnp.bfloat16)
            out[..., lane * 128 : (lane + 1) * 128] = piece.reshape(out.shape[:-1] + (128,))


def filter_and_transform(halo, voltages, window, table, groups, first, steps, before=()):
    inputs, samples = voltages.shape
    slots = samples // FFT_LEN
    rows = table.shape[0]
    widths = [part * CHANNELS // groups // EIGHTHS for part in PARTS]
    return pl.pallas_call(
        filter_kernel,
        grid=(steps,),
        in_specs=[
            pl.BlockSpec((inputs, HALO), lambda j: (0, 0)),
            pl.BlockSpec((inputs, STEP * FFT_LEN), lambda j: (0, j + first)),
            pl.BlockSpec((TAPS, FFT_LEN), lambda j: (0, 0)),
            pl.BlockSpec((rows, FFT_LEN), lambda j: (0, 0)),
        ]
        + [pl.BlockSpec(memory_space=pl.ANY)] * len(before),
        out_specs=[
            pl.BlockSpec((groups, width, 2, STEP, inputs), lambda j: (0, 0, 0, j + first, 0)) for width in widths
        ],
        out_shape=[jax.ShapeDtypeStruct((groups, width, 2, slots, inputs), jnp.bfloat16) for width in widths],
        input_output_aliases={4 + chunk: chunk for chunk in range(len(before))},
        cost_estimate=pl.CostEstimate(
            flops=2 * rows * FFT_LEN * inputs * steps * STEP * 4,
            bytes_accessed=4 * steps * STEP * FFT_LEN * inputs,
            transcendentals=0,
        ),
        scratch_shapes=[
            pltpu.VMEM((inputs, HALO + STEP * FFT_LEN), jnp.bfloat16),
            pltpu.VMEM((inputs, FFT_LEN), jnp.bfloat16),
            pltpu.VMEM((inputs // 128, rows * STEP, 128), jnp.float32),
        ],
        compiler_params=pltpu.CompilerParams(vmem_limit_bytes=50 * 2**20),
        name="filter_and_transform",
    )(halo, voltages, window, table, *before)


def tile_kernel(scale, place_ref, left_ref, right_ref, *rest):
    out = rest[-1]
    devices, _, _, parts, slots, inputs = left_ref.shape

    def matrix(ref, index, part):
        return ref[:, index, 0, part].reshape(devices * slots, inputs)

    def product(left, right):
        return lax.dot_general(left, right, (((0,), (0,)), ((), ())), preferred_element_type=jnp.float32)

    for i in range(left_ref.shape[1]):
        rows = slice(i * inputs, (i + 1) * inputs)
        left = [matrix(left_ref, i, 0), matrix(left_ref, i, 1)]
        for j in range(right_ref.shape[1]):
            columns = slice(j * inputs, (j + 1) * inputs)
            right = [matrix(right_ref, j, 0), matrix(right_ref, j, 1)]
            out[0, 0, rows, columns] = (product(left[0], right[0]) + product(left[1], right[1])) * scale
            out[0, 1, rows, columns] = (product(left[1], right[0]) - product(left[0], right[1])) * scale


def tiles(piece, place, before, start, shape, scale):
    devices, groups, width, parts, slots, inputs = piece.shape
    rows, columns = shape[2] // inputs, shape[3] // inputs
    in_specs = [
        pl.BlockSpec((devices, rows, 1, parts, slots, inputs), lambda k, at: (0, at[0], k, 0, 0, 0)),
        pl.BlockSpec((devices, columns, 1, parts, slots, inputs), lambda k, at: (0, at[1], k, 0, 0, 0)),
    ]
    operands = [place, piece, piece]
    aliases = {}
    if before is not None:
        in_specs.append(pl.BlockSpec(memory_space=pl.ANY))
        operands.append(before)
        aliases = {3: 0}
    moved = (rows + columns) * devices * width * parts * slots * inputs * 2
    return pl.pallas_call(
        functools.partial(tile_kernel, scale),
        grid_spec=pltpu.PrefetchScalarGridSpec(
            num_scalar_prefetch=1,
            grid=(width,),
            in_specs=in_specs,
            out_specs=pl.BlockSpec((1,) + shape[1:], lambda k, at: (start + k, 0, 0, 0)),
        ),
        out_shape=jax.ShapeDtypeStruct(shape, jnp.float32),
        input_output_aliases=aliases,
        cost_estimate=pl.CostEstimate(
            flops=8 * width * devices * slots * shape[2] * shape[3],
            bytes_accessed=moved + width * 2 * shape[2] * shape[3] * 4,
            transcendentals=0,
        ),
        compiler_params=pltpu.CompilerParams(vmem_limit_bytes=56 * 2**20),
        name="visibility_tiles",
    )(*operands)


def chunked(voltages):
    samples = voltages.shape[1]
    groups = lax.axis_size("chan")
    table = fourier_table(CHANNELS, FFT_LEN)
    table = table.reshape(groups, EIGHTHS, CHANNELS // groups // EIGHTHS, 2, FFT_LEN)
    ends = [sum(PARTS[: chunk + 1]) for chunk in range(len(PARTS))]
    table = [table[:, end - part : end].reshape(-1, FFT_LEN) for end, part in zip(ends, PARTS)]
    table = jnp.concatenate(table, axis=0)
    window = window_table(TAPS, FFT_LEN)
    halo = shifted(voltages[:, samples - HALO :], ("row", "col"), 1)
    steps = samples // (STEP * FFT_LEN)
    own = voltages[:, STEP * FFT_LEN - HALO : STEP * FFT_LEN]
    chunks = filter_and_transform(own, voltages, window, table, groups, 1, steps - 1)
    chunks = filter_and_transform(halo, voltages, window, table, groups, 0, 1, chunks)
    row_count = lax.axis_size("row")
    col_count = lax.axis_size("col")
    total_inputs = voltages.shape[0] * groups
    spectra_total = samples // FFT_LEN * row_count * col_count
    place = jnp.stack([lax.axis_index("row"), lax.axis_index("col")]).astype(jnp.int32)
    shape = (CHANNELS // groups, 2, total_inputs // row_count, total_inputs // col_count)
    out, start = None, 0
    for chunk in chunks:
        turned = lax.all_to_all(chunk, "chan", split_axis=0, concat_axis=0, tiled=True)
        piece = lax.all_gather(turned, ("row", "col"), axis=0, tiled=False)
        out = tiles(piece, place, out, start, shape, 1.0 / spectra_total)
        start += chunk.shape[1]
    return out


def whole(voltages):
    local_inputs = voltages.shape[0]
    slot_spectra = voltages.shape[1] // FFT_LEN
    window = window_table(TAPS, FFT_LEN)
    table = fourier_table(CHANNELS, FFT_LEN)
    earlier = shifted(voltages[:, (slot_spectra - TAPS + 1) * FFT_LEN :], ("row", "col"), 1)
    extended = jnp.concatenate([earlier, voltages], axis=1).reshape(
        local_inputs, slot_spectra + TAPS - 1, FFT_LEN
    )
    total = jnp.zeros((local_inputs, slot_spectra, FFT_LEN), jnp.float32)
    for tap_index in range(TAPS):
        total = total + window[tap_index][None, None, :] * extended[
            :, tap_index : tap_index + slot_spectra, :
        ].astype(jnp.float32)
    filtered = total.astype(jnp.bfloat16)
    spectra = jnp.einsum(
        "kpn,isn->kpsi", table, filtered, preferred_element_type=jnp.float32
    ).astype(jnp.bfloat16)
    turned = lax.all_to_all(spectra, "chan", split_axis=0, concat_axis=3, tiled=True)
    inputs_all = turned.shape[3]
    row_count = lax.axis_size("row")
    col_count = lax.axis_size("col")
    row_block = inputs_all // row_count
    col_block = inputs_all // col_count
    spectra_total = slot_spectra * row_count * col_count
    piece = lax.all_gather(turned, ("row", "col"), axis=2, tiled=True)
    left = lax.dynamic_slice_in_dim(piece, lax.axis_index("row") * row_block, row_block, 3)
    right = lax.dynamic_slice_in_dim(piece, lax.axis_index("col") * col_block, col_block, 3)
    flipped = jnp.stack([left[:, 1], -left[:, 0]], axis=1)
    real_part = jnp.einsum("cpsi,cpsj->cij", left, right, preferred_element_type=jnp.float32)
    imag_part = jnp.einsum("cpsi,cpsj->cij", flipped, right, preferred_element_type=jnp.float32)
    return jnp.stack([real_part, imag_part], axis=1) / spectra_total


def per_device(voltages):
    inputs, samples = voltages.shape
    groups = lax.axis_size("chan")
    row_block = inputs * groups // lax.axis_size("row")
    col_block = inputs * groups // lax.axis_size("col")
    fits = inputs % 128 == 0 and row_block % inputs == 0 and col_block % inputs == 0
    fits = fits and CHANNELS % (groups * EIGHTHS) == 0 and samples % (STEP * FFT_LEN) == 0
    fits = fits and samples > STEP * FFT_LEN
    return chunked(voltages) if fits else whole(voltages)


def solution(mesh):
    placed = (P("chan", ("row", "col")),)
    return jax.shard_map(
        per_device,
        mesh=mesh,
        in_specs=placed,
        out_specs=P("chan", None, "row", "col"),
        check_vma=False,
    )
```
